512 devices in a mesh: ctx: 64 (over z, y), resp: 8 (over x, core).
Axes of the slice: x: 4, y: 8, z: 8, core: 2. Of those that a mesh axis runs over, the one named last changes fastest.
Arguments:
- queries: bfloat16 [64, 128, 8192], P('resp', None, 'ctx'), may hold values from -70 to 70
- keys: bfloat16 [32768, 1024], P('ctx'), may hold values from -40.5 to 40.5
- values: bfloat16 [32768, 1024], P('ctx'), may hold values from -48 to 48
- span_ids: int32 [64, 2], P('resp'), may hold values from 0 to 15, all different within a row; in each aligned block of 8 rows (0 to 7, 8 to 15, ...) at most 2 rows name the same one
- lengths: int32 [64], P('resp'), may hold values from 1 to 2
- judge: float32 [8192], replicated, may hold values from -1 to 1
Outputs:
- attended: bfloat16 [64, 128, 8192], P('resp', None, 'ctx')
- relative: float32 [64], replicated
The draws below stay inside these ranges and needn't reach their ends.
Inputs may be any that keep to these rules, and one draw needn't show every extreme that they name: `span_ids`: each response names 2 different spans. Among the 8 responses of one group (aligned blocks of rows) no span is named by more than 2 responses, a bound that some block reaches.
All inputs are finite; a program needn't handle non-finite values.
Results may differ from the reference program's by a relative error of at most 0.0059.
Values may be sent and summed in bfloat16 or wider, within the bound.
A program may use at most 64 MiB of HBM per device.

```python
import math
import jax
import jax.numpy as jnp
import numpy as np
from jax import lax

QUERY_HEADS = 64
KEY_HEADS = 8
HEAD_WIDTH = 128
W = 8192
KW = 1024
SPAN_LENGTH = 2048
LOCAL_DOC_LENGTH = 512
DOCUMENT_LENGTH = 32768
SPAN_TOTAL = 16
RESPONSE_LENGTH = 128
BLK = 64
RBLK = 2
PICKED_SPANS = 2
R_GRP = 8
RESPONSES = 64
MOST = 2


def draw_queries(key, part):
    key = jax.random.fold_in(key, 11)
    sampled_draw = 2.0 * jax.random.normal(key, (RESPONSES, RESPONSE_LENGTH, QUERY_HEADS, HEAD_WIDTH), jnp.float32)
    return sampled_draw.reshape(RESPONSES, RESPONSE_LENGTH, QUERY_HEADS * HEAD_WIDTH).astype(jnp.bfloat16)


def draw_keys(key, part):
    key = jax.random.fold_in(key, 23)
    sampled_draw = jax.random.normal(key, (DOCUMENT_LENGTH, KEY_HEADS, HEAD_WIDTH), jnp.float32)
    return sampled_draw.reshape(DOCUMENT_LENGTH, KEY_HEADS * HEAD_WIDTH).astype(jnp.bfloat16)


def place_ends(values, stream_key, smallest, top_value):
    extent = values.shape
    spot = [jax.random.randint(jax.random.fold_in(stream_key, axis), (), 0, extent[axis]) for axis in range(len(extent))]
    values = values.at[tuple(spot)].set(smallest)
    longest = extent.index(max(extent))
    spot[longest] = (spot[longest] + 1) % extent[longest]
    return values.at[tuple(spot)].set(top_value)


def block_levels(rng, shape, shards, low, largest):
    def one(position, parts):
        heights = jax.random.uniform(jax.random.fold_in(jax.random.fold_in(rng, 6), position), (parts,), jnp.float32, low / len(shards), largest / len(shards))
        return jnp.repeat(jnp.exp(heights), shape[position] // parts).reshape((-1,) + (1,) * (len(shape) - position - 1))

    loudness = one(*shards[0])
    for cut in shards[1:]:
        loudness = loudness * one(*cut)
    return loudness


def routed_block(own_key, own, number, rows, count, top, most, slope):
    ranking = jax.random.permutation(own_key, count)
    crowded, usual = load_shares(count, rows * top, most, slope, True), load_shares(count, rows * top, most, slope, False)
    places = jnp.arange(count)

    def named(tallies, rotation):
        used = int((tallies > 0).sum())
        fixed = max(1, used // 4)
        passed = fixed + (places - fixed + rotation * (used - fixed)) % max(1, count - fixed)
        return jnp.zeros((count,), jnp.int32).at[ranking[jnp.where(places < fixed, places, passed)]].set(jnp.asarray(tallies, jnp.int32))

    tallies = jnp.where(number % 4 == 0, named(crowded, number // 4), named(usual, number - number // 4 - 1))
    mixed = jax.random.permutation(jax.random.fold_in(own, 3), count)
    giver, sink = mixed[0:count // 2 * 2:2], mixed[1:count // 2 * 2:2]
    slack = jnp.minimum(tallies[giver] - 1, most - tallies[sink]) // 2
    slack = jnp.where((giver == ranking[0]) | (sink == ranking[0]) | (tallies[sink] == 0), 0, jnp.maximum(slack, 0))
    passed = jax.random.randint(jax.random.fold_in(own, 4), (count // 2,), 0, 1 << 20) % (slack + 1)
    tallies = tallies.at[giver].add(-passed).at[sink].add(passed)
    items = jnp.searchsorted(jnp.cumsum(tallies), jnp.arange(rows * top), side="right").astype(jnp.int32)
    listing = items.reshape(top, rows).T
    listing = listing[jax.random.permutation(jax.random.fold_in(own, 1), rows)]
    rotation = jax.random.randint(jax.random.fold_in(own, 2), (rows, 1), 0, top)
    return jnp.take_along_axis(listing, (jnp.arange(top)[None, :] + rotation) % top, axis=1)


def load_shares(amount, total, bound, lean, full):
    loads = [(1 << 20) // math.isqrt(standing ** lean) + 1 for standing in range(1, amount + 1)]
    largest = bound if full else min(bound, max(-(-total // amount), total * loads[0] // sum(loads)))
    least = 1 if total - largest >= amount - 1 else 0
    given, rest = [largest] + [least] * (amount - 1), total - largest - least * (amount - 1)
    while rest > 0:
        movable = [i for i in range(1, amount) if given[i] < largest] or [i for i in range(1, amount) if given[i] < bound]
        whole, budget = sum([loads[i] for i in movable]), rest
        for i in movable:
            more = min(bound - given[i], max(1, budget * loads[i] // whole), rest)
            given[i] = given[i] + more
            rest = rest - more
    return np.array(given)


def gaussian(key, dims, width, reach, split=(), kind=jnp.bfloat16):
    factor_of = block_levels(key, dims, split, -0.22, 0.18) if split else 1.0
    array = jax.random.normal(key, dims, jnp.float32) * width * factor_of
    return jnp.minimum(jnp.maximum(array, -reach), reach).astype(kind)


def setup_inputs(seed: int = 0) -> dict:
    seeds = jax.random.split(jax.random.key(seed), 7)
    queries = draw_queries(jax.random.fold_in(seeds[6], 71), 0)
    keys = draw_keys(jax.random.fold_in(seeds[6], 71), 0)
    values = gaussian(seeds[2], (DOCUMENT_LENGTH, KW), 8.0, 48.0, ((0, 64),))
    span_ids_keys = jax.random.split(jax.random.fold_in(seeds[3], 1), RESPONSES // R_GRP)
    span_ids_turns = jax.random.permutation(jax.random.fold_in(seeds[3], 3), RESPONSES // R_GRP)
    span_ids = jax.vmap(lambda own, number: routed_block(jax.random.fold_in(seeds[3], 2), own, number, R_GRP, SPAN_TOTAL, PICKED_SPANS, MOST, 2))(span_ids_keys, span_ids_turns).reshape((RESPONSES, PICKED_SPANS))
    lengths = place_ends(jax.random.randint(seeds[4], (RESPONSES,), 1, RBLK + 1), jax.random.fold_in(seeds[4], 1), 1, RBLK).astype(jnp.int32)
    judge = gaussian(seeds[5], (W,), (max(1, W // 256)) ** -0.5, 1.0, (), jnp.float32)
    return {"queries": queries, "keys": keys, "values": values, "span_ids": span_ids, "lengths": lengths, "judge": judge}


def reference(queries, keys, values, span_ids, lengths, judge):
    queries_per_group = QUERY_HEADS // KEY_HEADS
    span_fragments = SPAN_LENGTH // LOCAL_DOC_LENGTH
    inverse = 1.0 / math.sqrt(HEAD_WIDTH)
    key_span_blocks = keys.reshape(SPAN_TOTAL, SPAN_LENGTH, KEY_HEADS, HEAD_WIDTH)
    value_span_blocks = values.reshape(SPAN_TOTAL, SPAN_LENGTH, KEY_HEADS, HEAD_WIDTH)
    highest = lax.Precision.HIGHEST

    def one_response(packed):
        query_rows, picked_span_index, length = packed
        query_floats = query_rows.reshape(RESPONSE_LENGTH, KEY_HEADS, queries_per_group, HEAD_WIDTH).astype(jnp.float32)
        key_floats = jnp.take(key_span_blocks, picked_span_index.astype(jnp.int32), axis=0).reshape(PICKED_SPANS * span_fragments, LOCAL_DOC_LENGTH, KEY_HEADS, HEAD_WIDTH).astype(jnp.float32)
        value_floats = jnp.take(value_span_blocks, picked_span_index.astype(jnp.int32), axis=0).reshape(PICKED_SPANS * span_fragments, LOCAL_DOC_LENGTH, KEY_HEADS, HEAD_WIDTH).astype(jnp.float32)
        scores = jnp.einsum('tgjd,npgd->gjtnp', query_floats, key_floats, precision=highest) * inverse
        shard_max = scores.max(-1).astype(jnp.bfloat16)
        shard_max = lax.optimization_barrier(shard_max).astype(jnp.float32)
        expo = jnp.exp(scores - shard_max[..., None])
        shard_total = lax.optimization_barrier(jnp.sum(expo, axis=-1)).astype(jnp.bfloat16)
        shard_total = lax.optimization_barrier(shard_total).astype(jnp.float32)
        probs = lax.optimization_barrier(expo.astype(jnp.bfloat16)).astype(jnp.float32)
        shard_out = jnp.einsum('gjtnp,npgd->gjtnd', probs, value_floats, precision=highest).astype(jnp.bfloat16)
        shard_out = lax.optimization_barrier(shard_out).astype(jnp.float32)
        top = shard_max.max(-1)
        rescale = jnp.exp(shard_max - top[..., None])
        numer = lax.optimization_barrier(jnp.sum(rescale[..., None] * shard_out, axis=3))
        denom = lax.optimization_barrier(jnp.sum(rescale * shard_total, axis=-1))
        result = numer / denom[..., None]
        result = jnp.transpose(result, (2, 0, 1, 3)).reshape(RESPONSE_LENGTH, QUERY_HEADS * HEAD_WIDTH)
        live = jnp.arange(RESPONSE_LENGTH, dtype=jnp.int32) < BLK * length
        return jnp.where(live[:, None], result, 0.0).astype(jnp.bfloat16)
    attended = lax.map(one_response, (queries, span_ids, lengths))
    dots = jnp.einsum('rtw,w->rt', attended.astype(jnp.float32), judge, precision=highest)
    live = jnp.arange(RESPONSE_LENGTH, dtype=jnp.int32)[None, :] < BLK * lengths[:, None]
    score = lax.optimization_barrier(jnp.sum(jnp.where(live, dots, 0.0), axis=1)) / (BLK * lengths).astype(jnp.float32)
    relative = score - jnp.mean(score)
    return (attended, relative)
```

```python
import math

import jax
import jax.numpy as jnp
from jax import lax
from jax.experimental import pallas as pl
from jax.experimental.pallas import tpu as pltpu
from jax.sharding import PartitionSpec as P

MESH = pl.DeviceIdType.MESH
NZ, NY, NX, NC = 8, 8, 4, 2
NG = NX * NC
HEAD = 128
TOK = 128
RESP = 8
BLK = 64
POS = 64
SCALE = math.log2(math.e) / math.sqrt(HEAD)
BF = jnp.bfloat16
F32 = jnp.float32


def kernel(
    q_ref, k_ref, v_ref, span_ref, len_ref, judge_ref,
    att_ref, rel_ref,
    kbuf, vbuf, vstage, vtb, qbuf, idbuf, idsm, pbuf, sstat, rstat, obuf, rbuf, t1, t2, t3,
    local_sem, zsend, zrecv, ysend, yrecv, csend, crecv, qsend, qrecv, idsend, idrecv,
    ssend, srecv, osend, orecv, rsend, rrecv,
):
    n = lax.axis_index("ctx")
    g = lax.axis_index("resp")
    z, y = n // NY, n % NY
    x, c = g // NC, g % NC
    half, quarter = y // 4, y % 4

    def at_z(zz):
        return (zz * NY + y, g)

    def at_y(yy):
        return (z * NY + yy, g)

    def at_g(gg):
        return (n, gg)

    def remote(src, dst, ss, rs, dev):
        return pltpu.make_async_remote_copy(
            src_ref=src, dst_ref=dst, send_sem=ss, recv_sem=rs, device_id=dev, device_id_type=MESH
        )

    sent = []

    def send(src, dst, ss, rs, dev):
        copy = remote(src, dst, ss, rs, dev)
        copy.start()
        sent.append(copy)

    def arrived(dst, rs):
        remote(dst, dst, rs, rs, at_g(g)).wait_recv()

    rows = pl.ds(pl.multiple_of(x * 128, 128), 128)
    krows = pl.ds(pl.multiple_of(x * 128 + c * POS, POS), POS)

    def cols(zz):
        return pl.ds(pl.multiple_of(zz * HEAD, HEAD), HEAD)

    vload = pltpu.make_async_copy(v_ref.at[rows, :], vstage, local_sem.at[0])
    vload.start()
    kown = pltpu.make_async_copy(
        k_ref.at[krows, cols(z)], kbuf.at[z, half, quarter, c], local_sem.at[1]
    )
    kown.start()
    qown = pltpu.make_async_copy(q_ref, qbuf.at[0], local_sem.at[2])
    qown.start()
    idbuf[0] = span_ref[...]

    barrier = pltpu.get_barrier_semaphore()
    for d in range(1, NZ):
        pl.semaphore_signal(barrier, inc=1, device_id=at_z((z + d) % NZ), device_id_type=MESH)
    for d in range(1, NY):
        pl.semaphore_signal(barrier, inc=1, device_id=at_y((y + d) % NY), device_id_type=MESH)
    for d in range(1, NG):
        pl.semaphore_signal(barrier, inc=1, device_id=at_g((g + d) % NG), device_id_type=MESH)
    pl.semaphore_wait(barrier, NZ + NY + NG - 3)

    for d in range(1, NZ):
        zz = (z + d) % NZ
        send(
            k_ref.at[krows, cols(zz)], kbuf.at[z, half, quarter, c],
            zsend.at[0, d], zrecv.at[0, d], at_z(zz),
        )
    for d in (2, 1, 3):
        dev = at_g(((x + d) % NX) * NC + c)
        send(idbuf.at[0], idbuf.at[4 - d], idsend.at[d], idrecv.at[4 - d], dev)
        send(q_ref, qbuf.at[4 - d], qsend.at[d], qrecv.at[4 - d], dev)
    vload.wait()
    for j in range(NZ):
        vtb[j] = jnp.transpose(vstage[:, j * HEAD:(j + 1) * HEAD]).reshape(2, POS, 128)
    vbuf[z, half, quarter, c] = vtb[z, c]
    for d in range(1, NZ):
        zz = (z + d) % NZ
        send(
            vtb.at[zz, c], vbuf.at[z, half, quarter, c],
            zsend.at[1, d], zrecv.at[1, d], at_z(zz),
        )

    bufs = (kbuf, vbuf)

    def piece(w, yy, p):
        return bufs[w].at[pl.ds(4 * p, 4), yy // 4, yy % 4, c]

    def valid(way, t, p):
        return t < 3 or p == way

    def to_next(w, way, t, p):
        yy = (y + (NY - t if way == 0 else t)) % NY
        dev = at_y((y + (1 if way == 0 else NY - 1)) % NY)
        ref = piece(w, yy, p)
        send(ref, ref, ysend.at[w, way, t, p], yrecv.at[w, way, t, p], dev)

    sibling = at_g(x * NC + (1 - c))

    def to_sibling(w, number, yy, p):
        ref = piece(w, yy, p)
        send(ref, ref, csend.at[w, number, p], crecv.at[w, number, p], sibling)

    def own_chunk(w):
        for d in range(1, NZ):
            arrived(bufs[w].at[(z + NZ - d) % NZ, half, quarter, c], zrecv.at[w, d])
        for p in range(2):
            for way in range(2):
                to_next(w, way, 0, p)
        for p in range(2):
            to_sibling(w, 0, y, p)

    def ring_step(w, t):
        for p in range(2):
            for way in range(2):
                if not valid(way, t, p):
                    continue
                yy = (y + (NY - 1 - t if way == 0 else 1 + t)) % NY
                arrived(piece(w, yy, p), yrecv.at[w, way, t, p])
                if t < 3 and valid(way, t + 1, p):
                    to_next(w, way, t + 1, p)
                to_sibling(w, (1 + 3 * way + t) if t < 3 else 7, yy, p)

    def from_sibling(w):
        for number in range(8):
            if number == 0:
                yy = y
            elif number < 4:
                yy = (y + NY - number) % NY
            elif number < 7:
                yy = (y + number - 3) % NY
            else:
                yy = (y + 4) % NY
            for p in range(2):
                arrived(
                    bufs[w].at[pl.ds(4 * p, 4), yy // 4, yy % 4, 1 - c], crecv.at[w, number, p]
                )

    kown.wait()
    own_chunk(0)
    own_chunk(1)
    for t in range(4):
        ring_step(0, t)
    qown.wait()
    for e in range(1, NX):
        arrived(idbuf.at[e], idrecv.at[e])
        arrived(qbuf.at[e], qrecv.at[e])
    ids = pltpu.make_async_copy(idbuf, idsm, local_sem.at[3])
    ids.start()
    ids.wait()
    from_sibling(0)

    def scores(e):
        def one(r, carry):
            q = qbuf[e, r]
            raw = []
            for k in range(2):
                s = idsm[e, r, k]
                keys = kbuf[s // 2, s % 2].reshape(512, HEAD)
                raw.append(
                    lax.dot_general(keys, q, (((1,), (1,)), ((), ())), preferred_element_type=F32)
                )
            top = jnp.maximum(
                jnp.max(raw[0], axis=0, keepdims=True), jnp.max(raw[1], axis=0, keepdims=True)
            )
            total = jnp.zeros((1, TOK), F32)
            for k in range(2):
                expo = jnp.exp2((raw[k] - top) * SCALE)
                total = total + jnp.sum(expo, axis=0, keepdims=True)
                pbuf[e, r, k] = expo.astype(BF)
            sstat[e, 0, pl.ds(r, 1), :] = top
            sstat[e, 1, pl.ds(r, 1), :] = total
            return carry

        lax.fori_loop(0, RESP, one, 0)

    for t, e in enumerate((2, 1, 3, 0)):
        ring_step(1, t)
        scores(e)
        if e:
            send(
                sstat.at[e], rstat.at[4 - e], ssend.at[e], srecv.at[4 - e],
                at_g(((x + e) % NX) * NC + c),
            )
    rstat[0] = sstat[0]
    from_sibling(1)

    def out_copy(e, r):
        return remote(
            obuf.at[e, r], rbuf.at[(4 - e) % 4, r], osend.at[e, r], orecv.at[(4 - e) % 4, r],
            at_g(((x + e) % NX) * NC + c),
        )

    def outputs(e):
        def one(r, carry):
            parts = []
            for k in range(2):
                s = idsm[e, r, k]
                vals = vbuf[s // 2, s % 2].reshape(4, HEAD, 128)
                parts += [vals[i] for i in range(4)]
            vt = jnp.concatenate(parts, axis=1)
            out = jnp.dot(vt, pbuf[e, r].reshape(1024, TOK), preferred_element_type=F32)
            out = (out * (1.0 / sstat[e, 1, pl.ds(r, 1), :])).astype(BF)
            if e:
                obuf[e, r] = out
                out_copy(e, r).start()
            else:
                rbuf[0, r] = out
            return carry

        lax.fori_loop(0, RESP, one, 0)

    for e in (2, 1, 3, 0):
        outputs(e)

    for e in range(1, NX):
        arrived(rstat.at[e], srecv.at[e])
    tops = rstat[:, 0]
    weight = jnp.exp2((tops - jnp.max(tops, axis=0, keepdims=True)) * SCALE) * rstat[:, 1]
    weight = weight / jnp.sum(weight, axis=0, keepdims=True)
    rstat[:, 0] = weight
    judge = jnp.transpose(jnp.broadcast_to(judge_ref[pl.ds(n, 1), :], (TOK, HEAD)))
    token = lax.broadcasted_iota(jnp.int32, (HEAD, TOK), 1)

    def combine(r, carry):
        total = jnp.zeros((HEAD, TOK), F32)
        for e in range(NX):
            if e:
                arrived(rbuf.at[e, r], orecv.at[e, r])
            total = total + rstat[e, 0, pl.ds(r, 1), :] * rbuf[e, r].astype(F32)
        total = jnp.where(token < BLK * len_ref[r], total, 0.0).astype(BF)
        att_ref[r] = jnp.transpose(total)
        t1[z, pl.ds(r, 1), :] = jnp.sum(total.astype(F32) * judge, axis=0, keepdims=True)
        return carry

    lax.fori_loop(0, RESP, combine, 0)

    def spread(number, buf, own, size, where):
        for d in range(1, size):
            send(
                buf.at[own], buf.at[own], rsend.at[number, d], rrecv.at[number, d],
                where((own + d) % size),
            )
        for d in range(1, size):
            arrived(buf.at[(own + size - d) % size], rrecv.at[number, d])

    spread(0, t1, z, NZ, at_z)
    t2[y] = jnp.sum(t1[...], axis=0)
    spread(1, t2, y, NY, at_y)
    dots = jnp.sum(jnp.sum(t2[...], axis=0), axis=1, keepdims=True)
    row = lax.broadcasted_iota(jnp.int32, (RESP, 128), 0)
    lane = lax.broadcasted_iota(jnp.int32, (RESP, 128), 1)
    tokens = jnp.ones((RESP, 128), F32)
    for r in range(RESP):
        tokens = jnp.where(row == r, (BLK * len_ref[r]).astype(F32), tokens)
    t3[g] = jnp.broadcast_to(dots, (RESP, 128)) / tokens
    spread(2, t3, g, NG, at_g)
    flat = jnp.zeros((RESP, 128), F32)
    for i in range(NG):
        flat = flat + jnp.where(lane == i * RESP + row, t3[i], 0.0)
    flat = jnp.sum(flat, axis=0, keepdims=True)
    rel_ref[...] = flat - jnp.sum(flat, axis=1, keepdims=True) / (NG * RESP)

    for copy in sent:
        copy.wait_send()

    def drain(r, carry):
        for e in range(1, NX):
            out_copy(e, r).wait_send()
        return carry

    lax.fori_loop(0, RESP, drain, 0)


def local(queries, keys, values, span_ids, lengths, judge):
    vmem = pl.BlockSpec(memory_space=pltpu.VMEM)
    smem = pl.BlockSpec(memory_space=pltpu.SMEM)
    hbm = pl.BlockSpec(memory_space=pl.ANY)
    dma = pltpu.SemaphoreType.DMA
    attended, relative = pl.pallas_call(
        kernel,
        out_shape=(
            jax.ShapeDtypeStruct((RESP, TOK, HEAD), BF),
            jax.ShapeDtypeStruct((1, 128), F32),
        ),
        in_specs=[hbm, hbm, hbm, vmem, smem, vmem],
        out_specs=(vmem, vmem),
        scratch_shapes=[
            pltpu.VMEM((NZ, 2, 4, 2, POS, HEAD), BF),
            pltpu.VMEM((NZ, 2, 4, 2, POS, 128), BF),
            pltpu.VMEM((128, NZ * HEAD), BF),
            pltpu.VMEM((NZ, 2, POS, 128), BF),
            pltpu.VMEM((NX, RESP, TOK, HEAD), BF),
            pltpu.VMEM((NX, RESP, 2), jnp.int32),
            pltpu.SMEM((NX, RESP, 2), jnp.int32),
            pltpu.VMEM((NX, RESP, 2, 512, TOK), BF),
            pltpu.VMEM((NX, 2, RESP, TOK), F32),
            pltpu.VMEM((NX, 2, RESP, TOK), F32),
            pltpu.VMEM((NX, RESP, HEAD, TOK), BF),
            pltpu.VMEM((NX, RESP, HEAD, TOK), BF),
            pltpu.VMEM((NZ, RESP, TOK), F32),
            pltpu.VMEM((NY, RESP, TOK), F32),
            pltpu.VMEM((NG, RESP, TOK), F32),
            dma((4,)),
            dma((2, NZ)),
            dma((2, NZ)),
            dma((2, 2, 4, 2)),
            dma((2, 2, 4, 2)),
            dma((2, 8, 2)),
            dma((2, 8, 2)),
            dma((NX,)),
            dma((NX,)),
            dma((NX,)),
            dma((NX,)),
            dma((NX,)),
            dma((NX,)),
            dma((NX, RESP)),
            dma((NX, RESP)),
            dma((3, 8)),
            dma((3, 8)),
        ],
        compiler_params=pltpu.CompilerParams(
            collective_id=0, has_side_effects=True, vmem_limit_bytes=40 * 1024 * 1024
        ),
    )(queries, keys, values, span_ids, lengths, judge.reshape(NZ * NY, HEAD))
    return attended, relative[0, :NG * RESP]


def solution(mesh):
    return jax.shard_map(
        local,
        mesh=mesh,
        in_specs=(
            P("resp", None, "ctx"),
            P("ctx", None),
            P("ctx", None),
            P("resp", None),
            P("resp"),
            P(),
        ),
        out_specs=(P("resp", None, "ctx"), P()),
        check_vma=False,
    )
```

```python
import math

import jax
import jax.numpy as jnp
from jax import lax
from jax.experimental import pallas as pl
from jax.experimental.pallas import tpu as pltpu
from jax.sharding import PartitionSpec as P

MESH = pl.DeviceIdType.MESH
NZ, NY, NX, NC = 8, 8, 4, 2
NG = NX * NC
HEAD = 128
TOK = 128
RESP = 8
BLK = 64
POS = 64
PIECES = (4, 2)
SCALE = math.log2(math.e) / math.sqrt(HEAD)
BF = jnp.bfloat16
F32 = jnp.float32


def kernel(
    q_ref, k_ref, v_ref, span_ref, len_ref, judge_ref,
    att_ref, rel_ref,
    kb0, kb1, kb2, kb3, vbuf, vstage, vtb, qbuf, idbuf, idsm, pbuf, mq, lq, coef, wmerge,
    sstat, rstat, mstat, obuf, mbuf, rbuf, jbuf, abuf, t1, t2, t3,
    local_sem, zsend, zrecv, ysend, yrecv, csend, crecv, qsend, qrecv, idsend, idrecv,
    ssend, srecv, osend, orecv, asem, rsend, rrecv,
):
    n = lax.axis_index("ctx")
    g = lax.axis_index("resp")
    z, y = n // NY, n % NY
    x, c = g // NC, g % NC
    half, quarter = y // 4, y % 4
    kb = (kb0, kb1, kb2, kb3)

    def at_z(zz):
        return (zz * NY + y, g)

    def at_y(yy):
        return (z * NY + yy, g)

    def at_g(gg):
        return (n, gg)

    def at_x(d):
        return (n, ((x + d) % NX) * NC + c)

    sibling = at_g(x * NC + (1 - c))

    def remote(src, dst, ss, rs, dev):
        return pltpu.make_async_remote_copy(
            src_ref=src, dst_ref=dst, send_sem=ss, recv_sem=rs, device_id=dev, device_id_type=MESH
        )

    sent = []

    def send(src, dst, ss, rs, dev):
        copy = remote(src, dst, ss, rs, dev)
        copy.start()
        sent.append(copy)

    def arrived(dst, rs):
        remote(dst, dst, rs, rs, sibling).wait_recv()

    def drain():
        while sent:
            sent.pop(0).wait_send()

    rows = pl.ds(pl.multiple_of(x * 128, 128), 128)
    krows = pl.ds(pl.multiple_of(x * 128 + c * POS, POS), POS)

    def cols(zz):
        return pl.ds(pl.multiple_of(zz * HEAD, HEAD), HEAD)

    vload = pltpu.make_async_copy(v_ref.at[rows, :], vstage, local_sem.at[0])
    vload.start()
    pltpu.make_async_copy(k_ref.at[krows, cols(z)], kb0.at[z, half, c], zrecv.at[0, 0]).start()
    idload = pltpu.make_async_copy(span_ref, idbuf.at[0], local_sem.at[1])
    idload.start()
    qown = pltpu.make_async_copy(q_ref, qbuf.at[0], local_sem.at[2])
    qown.start()
    jload = pltpu.make_async_copy(
        judge_ref.at[pl.ds(pl.multiple_of(z * NY, NY), NY), :], jbuf, local_sem.at[3]
    )
    jload.start()

    barrier = pltpu.get_barrier_semaphore()
    for d in range(1, NZ):
        pl.semaphore_signal(barrier, inc=1, device_id=at_z((z + d) % NZ), device_id_type=MESH)
    for d in range(1, NY):
        pl.semaphore_signal(barrier, inc=1, device_id=at_y((y + d) % NY), device_id_type=MESH)
    for d in range(1, NG):
        pl.semaphore_signal(barrier, inc=1, device_id=at_g((g + d) % NG), device_id_type=MESH)
    vload.wait()
    for j in range(NZ):
        vtb[j] = jnp.transpose(vstage[:, j * HEAD:(j + 1) * HEAD]).reshape(2, POS, 128)
    pltpu.make_async_copy(vtb.at[z, c], vbuf.at[z, half, quarter, c], zrecv.at[1, 0]).start()
    idload.wait()
    pl.semaphore_wait(barrier, NZ + NY + NG - 3)

    for d in (1, 7, 2, 6, 3, 5, 4):
        zz = (z + d) % NZ
        send(
            k_ref.at[krows, cols(zz)], kb0.at[z, half, c],
            zsend.at[0, d], zrecv.at[0, d], at_z(zz),
        )
    for d in (1, 7, 2, 6, 3, 5, 4):
        zz = (z + d) % NZ
        send(
            vtb.at[zz, c], vbuf.at[z, half, quarter, c],
            zsend.at[1, d], zrecv.at[1, d], at_z(zz),
        )
    for d in (1, 3, 2):
        send(idbuf.at[0], idbuf.at[4 - d], idsend.at[d], idrecv.at[4 - d], at_x(d))
    for d in (1, 3):
        send(q_ref, qbuf.at[4 - d], qsend.at[d], qrecv.at[4 - d], at_x(d))

    def chunk(w, j, zs, yy, cc):
        if w == 0:
            return kb[j % 4].at[zs, yy // 4, cc]
        return vbuf.at[zs, yy // 4, yy % 4, cc]

    def piece(w, j, i, cc):
        count = PIECES[w]
        width = NZ // count
        first = ((z // width + i) % count) * width
        return chunk(w, j, pl.ds(first, width), (y + j + NY) % NY, cc)

    def valid(w, way, t, i):
        return t < 3 or (i < PIECES[w] // 2) == (way == 0)

    def to_next(w, way, t, i):
        j = -t if way == 0 else t
        count = PIECES[w]
        width = NZ // count
        first = ((z // width + i) % count) * width
        dst = chunk(w, j + (-1 if way == 0 else 1), pl.ds(first, width), (y + j + NY) % NY, c)
        dev = at_y((y + (1 if way == 0 else NY - 1)) % NY)
        send(piece(w, j, i, c), dst, ysend.at[w, way, t, i], yrecv.at[w, way, t, i], dev)

    def to_sibling(w, number, j, i):
        ref = piece(w, j, i, c)
        send(ref, ref, csend.at[w, number, i], crecv.at[w, number, i], sibling)

    def own_chunk(w):
        count = PIECES[w]
        width = NZ // count
        for i in range(count):
            for k in range(width):
                zz = ((z // width + i) % count) * width + k
                arrived(chunk(w, 0, zz, y, c), zrecv.at[w, (z + NZ - zz) % NZ])
            for way in range(2):
                to_next(w, way, 0, i)
            to_sibling(w, 0, 0, i)

    def ring_step(w, t):
        for i in range(PIECES[w]):
            for way in range(2):
                if not valid(w, way, t, i):
                    continue
                j = -1 - t if way == 0 else 1 + t
                arrived(piece(w, j, i, c), yrecv.at[w, way, t, i])
                if t < 3 and valid(w, way, t + 1, i):
                    to_next(w, way, t + 1, i)
                to_sibling(w, (1 + 3 * way + t) if t < 3 else 7, j, i)

    def from_sibling(w, number):
        j = (0, -1, -2, -3, 1, 2, 3, 4)[number]
        for i in range(PIECES[w]):
            arrived(piece(w, j, i, 1 - c), crecv.at[w, number, i])

    def forward_queries():
        arrived(qbuf.at[1], qrecv.at[1])
        send(
            qbuf.at[1, pl.ds(4, 4)], qbuf.at[2, pl.ds(4, 4)], qsend.at[2], qrecv.at[2], at_x(3)
        )
        arrived(qbuf.at[3], qrecv.at[3])
        send(
            qbuf.at[3, pl.ds(0, 4)], qbuf.at[2, pl.ds(0, 4)], qsend.at[0], qrecv.at[0], at_x(1)
        )

    def wait_queries():
        qown.wait()
        arrived(qbuf.at[2, pl.ds(4, 4)], qrecv.at[2])
        arrived(qbuf.at[2, pl.ds(0, 4)], qrecv.at[0])
        for e in range(1, NX):
            arrived(idbuf.at[e], idrecv.at[e])
        ids = pltpu.make_async_copy(idbuf, idsm, local_sem.at[1])
        ids.start()
        ids.wait()

    def scores(j):
        def one(item, carry):
            e, r = item // RESP, item % RESP
            keys = []
            for k in range(2):
                s = idsm[e, k, r]
                keys.append(kb[j][s // 2, s % 2].reshape(128, HEAD))
            raw = lax.dot_general(
                jnp.concatenate(keys, axis=0), qbuf[e, r], (((1,), (1,)), ((), ())),
                preferred_element_type=F32,
            )
            top = jnp.max(raw, axis=0, keepdims=True)
            expo = jnp.exp2((raw - top) * SCALE)
            pbuf[e, r, j] = expo.astype(BF)
            mq[j, e, pl.ds(r, 1), :] = top
            lq[j, e, pl.ds(r, 1), :] = jnp.sum(expo, axis=0, keepdims=True)
            return carry

        lax.fori_loop(0, NX * RESP, one, 0, unroll=4)

    own_chunk(0)
    own_chunk(1)
    ring_step(0, 0)
    forward_queries()
    ring_step(1, 0)
    ring_step(0, 1)
    ring_step(1, 1)
    wait_queries()
    from_sibling(0, 2)
    from_sibling(0, 5)
    scores(2)
    ring_step(0, 2)
    ring_step(1, 2)
    for number in (1, 3, 4, 6):
        from_sibling(0, number)
    scores(1)
    scores(3)
    ring_step(0, 3)
    ring_step(1, 3)
    from_sibling(0, 0)
    from_sibling(0, 7)
    scores(0)

    row = lax.broadcasted_iota(jnp.int32, (RESP, 128), 0)
    for e in (2, 1, 3, 0):
        top = jnp.maximum(jnp.maximum(mq[0, e], mq[1, e]), jnp.maximum(mq[2, e], mq[3, e]))
        scale = [jnp.exp2((mq[j, e] - top) * SCALE) for j in range(4)]
        total = sum(scale[j] * lq[j, e] for j in range(4))
        sstat[e, 0] = top
        sstat[e, 1] = total
        if e:
            send(sstat.at[e], rstat.at[4 - e], ssend.at[e], srecv.at[4 - e], at_x(e))
        if e == 2:
            send(sstat.at[2], mstat.at[0], ssend.at[0], srecv.at[0], at_x(1))
            send(sstat.at[2], mstat.at[1], ssend.at[4], srecv.at[4], at_x(3))
        inverse = 1.0 / total
        for j in range(4):
            coef[e, j] = scale[j] * inverse
    rstat[0] = sstat[0]
    for number in range(8):
        from_sibling(1, number)

    def output(e, r):
        out = jnp.zeros((HEAD, TOK), F32)
        for j in range(4):
            vals = []
            for k in range(2):
                s = idsm[e, k, r]
                vals.append(vbuf[s // 2, s % 2, (quarter + j) % 4].reshape(HEAD, 128))
            part = jnp.dot(
                jnp.concatenate(vals, axis=1), pbuf[e, r, j], preferred_element_type=F32
            )
            out = out + part * coef[e, j, pl.ds(r, 1), :]
        return out

    def out_copy(e, r):
        if e == 2:
            return [
                remote(
                    obuf.at[2, rr], mbuf.at[rr], osend.at[2, rr], orecv.at[2, rr], at_x(d)
                )
                for rr, d in ((r, 1), (4 + r, 3))
            ]
        return remote(obuf.at[e, r], rbuf.at[4 - e, r], osend.at[e, r], orecv.at[4 - e, r], at_x(e))

    def opposite(r, carry):
        first, second = output(2, r), output(2, 4 + r)
        obuf[2, r] = first.astype(BF)
        obuf[2, 4 + r] = second.astype(BF)
        for copy in out_copy(2, r):
            copy.start()
        return carry

    def beside(r, carry):
        first, second = output(1, 4 + r), output(3, r)
        obuf[1, 4 + r] = first.astype(BF)
        obuf[3, r] = second.astype(BF)
        out_copy(1, 4 + r).start()
        out_copy(3, r).start()
        return carry

    def merged(r, carry):
        first, second = output(1, r), output(3, 4 + r)
        arrived(mbuf.at[r], orecv.at[2, r])
        arrived(mbuf.at[4 + r], orecv.at[2, 4 + r])
        first = first + mbuf[r].astype(F32) * wmerge[0, pl.ds(r, 1), :]
        second = second + mbuf[4 + r].astype(F32) * wmerge[1, pl.ds(4 + r, 1), :]
        obuf[1, r] = first.astype(BF)
        obuf[3, 4 + r] = second.astype(BF)
        out_copy(1, r).start()
        out_copy(3, 4 + r).start()
        return carry

    def mine(r, carry):
        first, second = output(0, r), output(0, 4 + r)
        rbuf[0, r] = first.astype(BF)
        rbuf[0, 4 + r] = second.astype(BF)
        return carry

    lax.fori_loop(0, 4, opposite, 0)
    lax.fori_loop(0, 4, beside, 0)
    arrived(mstat.at[0], srecv.at[0])
    arrived(mstat.at[1], srecv.at[4])
    for i, e in ((0, 1), (1, 3)):
        top = jnp.maximum(sstat[e, 0], mstat[i, 0])
        here = jnp.exp2((sstat[e, 0] - top) * SCALE) * sstat[e, 1]
        there = jnp.exp2((mstat[i, 0] - top) * SCALE) * mstat[i, 1]
        inverse = 1.0 / (here + there)
        wmerge[i] = there * inverse
        here = jnp.where((row < 4) == (i == 0), here * inverse, 1.0)
        for j in range(4):
            coef[e, j] = coef[e, j] * here
    lax.fori_loop(0, 4, merged, 0)
    lax.fori_loop(0, 4, mine, 0)

    for e in range(1, NX):
        arrived(rstat.at[e], srecv.at[e])
    tops = rstat[:, 0]
    weight = jnp.exp2((tops - jnp.max(tops, axis=0, keepdims=True)) * SCALE) * rstat[:, 1]
    weight = weight / jnp.sum(weight, axis=0, keepdims=True)
    rstat[0, 0] = weight[0]
    rstat[1, 0] = weight[1] + jnp.where(row < 4, 0.0, weight[2])
    rstat[3, 0] = weight[3] + jnp.where(row < 4, weight[2], 0.0)
    jload.wait()
    judge = jnp.transpose(jnp.broadcast_to(jbuf[pl.ds(y, 1), :], (TOK, HEAD)))
    token = lax.broadcasted_iota(jnp.int32, (HEAD, TOK), 1)

    def att_copy(r):
        return pltpu.make_async_copy(abuf.at[r], att_ref.at[r], asem.at[r])

    def combine(r):
        total = rstat[0, 0, pl.ds(r, 1), :] * rbuf[0, r].astype(F32)
        for e in (1, 3):
            arrived(rbuf.at[e, r], orecv.at[e, r])
            total = total + rstat[e, 0, pl.ds(r, 1), :] * rbuf[e, r].astype(F32)
        total = jnp.where(token < BLK * len_ref[r], total, 0.0).astype(BF)
        abuf[r] = jnp.transpose(total)
        att_copy(r).start()
        t1[z, pl.ds(r, 1), :] = jnp.sum(total.astype(F32) * judge, axis=0, keepdims=True)

    def combine_pair(r, carry):
        combine(r)
        combine(4 + r)
        return carry

    lax.fori_loop(0, 4, combine_pair, 0)

    def spread(number, buf, own, size, where):
        copies = []
        for d in range(1, size):
            copy = remote(
                buf.at[own], buf.at[own], rsend.at[number, d], rrecv.at[number, d],
                where((own + d) % size),
            )
            copy.start()
            copies.append(copy)
        drain()
        sent.extend(copies)
        for d in range(1, size):
            arrived(buf.at[(own + size - d) % size], rrecv.at[number, d])

    spread(0, t1, z, NZ, at_z)
    t2[y] = jnp.sum(t1[...], axis=0)
    spread(1, t2, y, NY, at_y)
    dots = jnp.sum(jnp.sum(t2[...], axis=0), axis=1, keepdims=True)
    lane = lax.broadcasted_iota(jnp.int32, (RESP, 128), 1)
    tokens = jnp.ones((RESP, 128), F32)
    for r in range(RESP):
        tokens = jnp.where(row == r, (BLK * len_ref[r]).astype(F32), tokens)
    t3[g] = jnp.broadcast_to(dots, (RESP, 128)) / tokens
    spread(2, t3, g, NG, at_g)
    flat = jnp.zeros((RESP, 128), F32)
    for i in range(NG):
        flat = flat + jnp.where(lane == i * RESP + row, t3[i], 0.0)
    flat = jnp.sum(flat, axis=0, keepdims=True)
    flat = flat - jnp.sum(flat, axis=1, keepdims=True) / (NG * RESP)
    rel_ref[...] = flat[:, :NG * RESP]
    drain()

    def finish(r, carry):
        for copy in out_copy(2, r):
            copy.wait_send()
        for rr in (r, 4 + r):
            out_copy(1, rr).wait_send()
            out_copy(3, rr).wait_send()
            att_copy(rr).wait()
        return carry

    lax.fori_loop(0, 4, finish, 0)


def local(queries, keys, values, span_ids, lengths, judge):
    vmem = pl.BlockSpec(memory_space=pltpu.VMEM)
    smem = pl.BlockSpec(memory_space=pltpu.SMEM)
    hbm = pl.BlockSpec(memory_space=pl.ANY)
    dma = pltpu.SemaphoreType.DMA
    attended, relative = pl.pallas_call(
        kernel,
        out_shape=(
            jax.ShapeDtypeStruct((RESP, TOK, HEAD), BF),
            jax.ShapeDtypeStruct((1, NG * RESP), F32),
        ),
        in_specs=[hbm, hbm, hbm, hbm, smem, hbm],
        out_specs=(hbm, vmem),
        scratch_shapes=[
            pltpu.VMEM((NZ, 2, 2, POS, HEAD), BF),
            pltpu.VMEM((NZ, 2, 2, POS, HEAD), BF),
            pltpu.VMEM((NZ, 2, 2, POS, HEAD), BF),
            pltpu.VMEM((NZ, 2, 2, POS, HEAD), BF),
            pltpu.VMEM((NZ, 2, 4, 2, POS, 128), BF),
            pltpu.VMEM((128, NZ * HEAD), BF),
            pltpu.VMEM((NZ, 2, POS, 128), BF),
            pltpu.VMEM((NX, RESP, TOK, HEAD), BF),
            pltpu.VMEM((NX, 2, RESP), jnp.int32),
            pltpu.SMEM((NX, 2, RESP), jnp.int32),
            pltpu.VMEM((NX, RESP, 4, 256, TOK), BF),
            pltpu.VMEM((4, NX, RESP, TOK), F32),
            pltpu.VMEM((4, NX, RESP, TOK), F32),
            pltpu.VMEM((NX, 4, RESP, TOK), F32),
            pltpu.VMEM((2, RESP, TOK), F32),
            pltpu.VMEM((NX, 2, RESP, TOK), F32),
            pltpu.VMEM((NX, 2, RESP, TOK), F32),
            pltpu.VMEM((2, 2, RESP, TOK), F32),
            pltpu.VMEM((NX, RESP, HEAD, TOK), BF),
            pltpu.VMEM((RESP, HEAD, TOK), BF),
            pltpu.VMEM((NX, RESP, HEAD, TOK), BF),
            pltpu.VMEM((NY, HEAD), F32),
            pltpu.VMEM((RESP, TOK, HEAD), BF),
            pltpu.VMEM((NZ, RESP, TOK), F32),
            pltpu.VMEM((NY, RESP, TOK), F32),
            pltpu.VMEM((NG, RESP, TOK), F32),
            dma((4,)),
            dma((2, NZ)),
            dma((2, NZ)),
            dma((2, 2, 4, 4)),
            dma((2, 2, 4, 4)),
            dma((2, 8, 4)),
            dma((2, 8, 4)),
            dma((NX,)),
            dma((NX,)),
            dma((NX,)),
            dma((NX,)),
            dma((5,)),
            dma((5,)),
            dma((NX, RESP)),
            dma((NX, RESP)),
            dma((RESP,)),
            dma((3, 8)),
            dma((3, 8)),
        ],
        compiler_params=pltpu.CompilerParams(
            collective_id=0, has_side_effects=True, vmem_limit_bytes=60 * 1024 * 1024
        ),
    )(queries, keys, values, span_ids.T, lengths, judge.reshape(NZ * NY, HEAD))
    return attended, relative.reshape(NG * RESP)


def solution(mesh):
    return jax.shard_map(
        local,
        mesh=mesh,
        in_specs=(
            P("resp", None, "ctx"),
            P("ctx", None),
            P("ctx", None),
            P("resp", None),
            P("resp"),
            P(),
        ),
        out_specs=(P("resp", None, "ctx"), P()),
        check_vma=False,
    )
```

```python
import math

import jax
import jax.numpy as jnp
from jax import lax
from jax.experimental import pallas as pl
from jax.experimental.pallas import tpu as pltpu
from jax.sharding import PartitionSpec as P

MESH = pl.DeviceIdType.MESH
NZ, NY, NX, NC = 8, 8, 4, 2
NG = NX * NC
HEAD = 128
TOK = 128
RESP = 8
BLK = 64
POS = 64
PIECES = (4, 4)
SCALE = math.log2(math.e) / math.sqrt(HEAD)
BF = jnp.bfloat16
F32 = jnp.float32


def kernel(
    q_ref, k_ref, v_ref, span_ref, len_ref, judge_ref,
    att_ref, rel_ref,
    kb0, kb1, kb2, kb3, vbuf, vstage, vtb, qbuf, idbuf, idsm, lens, pbuf, mq, lq, coef,
    sq, gstat, obuf, mbuf, rbuf, jbuf, vjs, vjr, vjt, vjf, vjb, abuf, t1, t2, t3,
    local_sem, zsend, zrecv, ysend, yrecv, csend, crecv, qsend, qrecv, idsend, idrecv,
    lsend, lrecv, jsend, jrecv, ssend, srecv, osend, orecv, asem, rsend, rrecv,
):
    n = lax.axis_index("ctx")
    g = lax.axis_index("resp")
    z, y = n // NY, n % NY
    x, c = g // NC, g % NC
    half, quarter = y // 4, y % 4
    kb = (kb0, kb1, kb2, kb3)

    def at_z(zz):
        return (zz * NY + y, g)

    def at_y(yy):
        return (z * NY + yy, g)

    def at_g(gg):
        return (n, gg)

    def at_x(d):
        return (n, ((x + d) % NX) * NC + c)

    sibling = at_g(x * NC + (1 - c))

    def remote(src, dst, ss, rs, dev):
        return pltpu.make_async_remote_copy(
            src_ref=src, dst_ref=dst, send_sem=ss, recv_sem=rs, device_id=dev, device_id_type=MESH
        )

    sent = []

    def send(src, dst, ss, rs, dev):
        copy = remote(src, dst, ss, rs, dev)
        copy.start()
        sent.append(copy)

    def arrived(dst, rs):
        remote(dst, dst, rs, rs, sibling).wait_recv()

    def drain():
        while sent:
            sent.pop(0).wait_send()

    rows = pl.ds(pl.multiple_of(x * 128, 128), 128)
    krows = pl.ds(pl.multiple_of(x * 128 + c * POS, POS), POS)

    def cols(zz):
        return pl.ds(pl.multiple_of(zz * HEAD, HEAD), HEAD)

    vload = pltpu.make_async_copy(v_ref.at[rows, :], vstage, local_sem.at[0])
    vload.start()
    pltpu.make_async_copy(k_ref.at[krows, cols(z)], kb0.at[z, half, c], zrecv.at[0, 0]).start()
    idload = pltpu.make_async_copy(span_ref, idbuf.at[0], local_sem.at[1])
    idload.start()
    qown = pltpu.make_async_copy(q_ref, qbuf.at[0], local_sem.at[2])
    qown.start()
    jload = pltpu.make_async_copy(judge_ref, jbuf, local_sem.at[3])
    jload.start()

    barrier = pltpu.get_barrier_semaphore()
    for d in range(1, NZ):
        pl.semaphore_signal(barrier, inc=1, device_id=at_z((z + d) % NZ), device_id_type=MESH)
    for d in range(1, NY):
        pl.semaphore_signal(barrier, inc=1, device_id=at_y((y + d) % NY), device_id_type=MESH)
    for d in range(1, NG):
        pl.semaphore_signal(barrier, inc=1, device_id=at_g((g + d) % NG), device_id_type=MESH)
    row = lax.broadcasted_iota(jnp.int32, (RESP, 128), 0)
    lane = lax.broadcasted_iota(jnp.int32, (RESP, 128), 1)
    own_lens = jnp.zeros((RESP, 128), jnp.int32)
    for r in range(RESP):
        own_lens = jnp.where(row == r, len_ref[r], own_lens)
    pl.semaphore_wait(barrier, NZ + NY + NG - 3)

    for d in (1, 7, 2, 6, 3, 5, 4):
        zz = (z + d) % NZ
        send(
            k_ref.at[krows, cols(zz)], kb0.at[z, half, c],
            zsend.at[0, d], zrecv.at[0, d], at_z(zz),
        )
    for i in range(2):
        for d in (1, 3):
            part = pl.ds(4 * i if d == 1 else 4 - 4 * i, 4)
            send(
                q_ref.at[part], qbuf.at[4 - d, part], qsend.at[d, i], qrecv.at[4 - d, i], at_x(d)
            )
    vload.wait()
    for j in range(NZ):
        vtb[j] = jnp.transpose(vstage[:, j * HEAD:(j + 1) * HEAD]).reshape(2, POS, 128)
    pltpu.make_async_copy(vtb.at[z, c], vbuf.at[z, half, quarter, c], zrecv.at[1, 0]).start()
    for d in (1, 7, 2, 6, 3, 5, 4):
        zz = (z + d) % NZ
        send(
            vtb.at[zz, c], vbuf.at[z, half, quarter, c],
            zsend.at[1, d], zrecv.at[1, d], at_z(zz),
        )
    jload.wait()
    for j in range(NZ):
        rest = jbuf[j * NY:(j + 1) * NY, :]
        terms = []
        for _ in range(3):
            terms.append(rest.astype(BF).astype(F32))
            rest = rest - terms[-1]
        terms.append(jnp.zeros((NY, HEAD), F32))
        dots = jnp.dot(
            jnp.concatenate(terms, axis=0).astype(BF), vtb[j].reshape(HEAD, 128),
            preferred_element_type=F32,
        )
        vjs[j] = dots[:NY] + dots[NY:2 * NY] + dots[2 * NY:3 * NY]
    vjr[z] = vjs[z]
    for d in range(1, NZ):
        zz = (z + d) % NZ
        send(vjs.at[zz], vjr.at[z], jsend.at[0, d], jrecv.at[0, d], at_z(zz))
    idload.wait()
    lens[0] = own_lens * BLK
    for d in (1, 3, 2):
        send(idbuf.at[0], idbuf.at[4 - d], idsend.at[d], idrecv.at[4 - d], at_x(d))
        send(lens.at[0], lens.at[4 - d], lsend.at[d], lrecv.at[4 - d], at_x(d))

    def chunk(w, j, zs, yy, cc):
        if w == 0:
            return kb[j % 4].at[zs, yy // 4, cc]
        return vbuf.at[zs, yy // 4, yy % 4, cc]

    def piece(w, j, i, cc):
        count = PIECES[w]
        width = NZ // count
        first = ((z // width + i) % count) * width
        return chunk(w, j, pl.ds(first, width), (y + j + NY) % NY, cc)

    def valid(w, way, t, i):
        return t < 3 or (i < PIECES[w] // 2) == (way == 0)

    def to_next(w, way, t, i):
        j = -t if way == 0 else t
        count = PIECES[w]
        width = NZ // count
        first = ((z // width + i) % count) * width
        dst = chunk(w, j + (-1 if way == 0 else 1), pl.ds(first, width), (y + j + NY) % NY, c)
        dev = at_y((y + (1 if way == 0 else NY - 1)) % NY)
        send(piece(w, j, i, c), dst, ysend.at[w, way, t, i], yrecv.at[w, way, t, i], dev)

    def to_sibling(w, number, j, i):
        ref = piece(w, j, i, c)
        send(ref, ref, csend.at[w, number, i], crecv.at[w, number, i], sibling)

    def own_chunk(w):
        count = PIECES[w]
        width = NZ // count
        for i in range(count):
            for k in range(width):
                zz = ((z // width + i) % count) * width + k
                arrived(chunk(w, 0, zz, y, c), zrecv.at[w, (z + NZ - zz) % NZ])
            for way in range(2):
                to_next(w, way, 0, i)
            to_sibling(w, 0, 0, i)

    def ring_step(w, t, work=()):
        work = list(work)
        for i in range(PIECES[w]):
            if i % 2 == 0 and work:
                work.pop(0)()
            for way in range(2):
                if not valid(w, way, t, i):
                    continue
                j = -1 - t if way == 0 else 1 + t
                arrived(piece(w, j, i, c), yrecv.at[w, way, t, i])
                if t < 3 and valid(w, way, t + 1, i):
                    to_next(w, way, t + 1, i)
                to_sibling(w, (1 + 3 * way + t) if t < 3 else 7, j, i)

    def from_sibling(w, number):
        j = (0, -1, -2, -3, 1, 2, 3, 4)[number]
        for i in range(PIECES[w]):
            arrived(piece(w, j, i, 1 - c), crecv.at[w, number, i])

    def forward_queries():
        for d in (1, 3):
            part = pl.ds(4 if d == 1 else 0, 4)
            arrived(qbuf.at[d, part], qrecv.at[d, 0])
            send(
                qbuf.at[d, part], qbuf.at[2, part], qsend.at[2, d // 2], qrecv.at[2, d // 2],
                at_x(4 - d),
            )

    def wait_queries():
        qown.wait()
        for d in (1, 3):
            arrived(qbuf.at[d, pl.ds(0 if d == 1 else 4, 4)], qrecv.at[d, 1])
            arrived(qbuf.at[2, pl.ds(4 if d == 1 else 0, 4)], qrecv.at[2, d // 2])
        for e in range(1, NX):
            arrived(idbuf.at[e], idrecv.at[e])
            arrived(lens.at[e], lrecv.at[e])
        ids = pltpu.make_async_copy(idbuf, idsm, local_sem.at[1])
        ids.start()
        ids.wait()

    def judged_to_heads():
        for d in range(1, NZ):
            arrived(vjr.at[(z + NZ - d) % NZ], jrecv.at[0, d])
        for yy in range(NY):
            vjt[yy] = vjr[:, yy, :]
        vjf[y] = vjt[y]
        for d in range(1, NY):
            yy = (y + d) % NY
            send(vjt.at[yy], vjf.at[y], jsend.at[1, d], jrecv.at[1, d], at_y(yy))

    def judged_values():
        for d in range(1, NY):
            arrived(vjf.at[(y + NY - d) % NY], jrecv.at[1, d])
        line = lax.broadcasted_iota(jnp.int32, (16, 128), 0)

        def one(zz, carry):
            for yy in range(NY):
                exact = jnp.broadcast_to(vjf[yy, pl.ds(zz, 1), :], (16, 128))
                high = exact.astype(BF).astype(F32)
                j = 2 * ((yy % 4 - quarter + 4) % 4)
                tile = jnp.where(line == j, high, jnp.where(line == j + 1, exact - high, 0.0))
                vjb[zz, yy // 4, yy % 4] = tile.astype(BF)
            return carry

        lax.fori_loop(0, NZ, one, 0)

    def scores(j, part):
        def one(item, carry):
            e, r = item // RESP, item % RESP
            keys = []
            for k in range(2):
                s = idsm[e, k, r]
                keys.append(kb[j][s // 2, s % 2].reshape(128, HEAD))
            raw = lax.dot_general(
                jnp.concatenate(keys, axis=0), qbuf[e, r], (((1,), (1,)), ((), ())),
                preferred_element_type=F32,
            )
            top = jnp.max(raw, axis=0, keepdims=True)
            expo = jnp.exp2((raw - top) * SCALE)
            pbuf[e, r, j] = expo.astype(BF)
            mq[j, e, pl.ds(r, 1), :] = top
            lq[j, e, pl.ds(r, 1), :] = jnp.sum(expo, axis=0, keepdims=True)
            return carry

        lax.fori_loop(16 * part, 16 * part + 16, one, 0, unroll=8)

    def both(j):
        return [lambda: scores(j, 0), lambda: scores(j, 1)]

    def spread(number, buf, own, size, where):
        for d in range(1, size):
            send(
                buf.at[own], buf.at[own], rsend.at[number, d], rrecv.at[number, d],
                where((own + d) % size),
            )

    def gather(number, buf, own, size):
        for d in range(1, size):
            arrived(buf.at[(own + size - d) % size], rrecv.at[number, d])

    def probe(part):
        def one(item, carry):
            e, r = item // RESP, item % RESP
            probes = []
            for j in range(4):
                for k in range(2):
                    s = idsm[e, k, r]
                    probes.append(vjb[s // 2, s % 2, (quarter + j) % 4])
            dots = jnp.dot(
                jnp.concatenate(probes, axis=1), pbuf[e, r].reshape(1024, TOK),
                preferred_element_type=F32,
            )
            for j in range(4):
                sq[j, e, pl.ds(r, 1), :] = dots[2 * j:2 * j + 1] + dots[2 * j + 1:2 * j + 2]
            return carry

        lax.fori_loop(16 * part, 16 * part + 16, one, 0, unroll=4)

    own_chunk(0)
    forward_queries()
    ring_step(0, 0)
    judged_to_heads()
    own_chunk(1)
    ring_step(0, 1)
    wait_queries()
    ring_step(1, 0)
    from_sibling(0, 2)
    from_sibling(0, 5)
    ring_step(0, 2, both(2))
    judged_values()
    ring_step(1, 1)
    for number in (1, 3, 4, 6):
        from_sibling(0, number)
    ring_step(0, 3, both(1))
    scores(3, 0)
    ring_step(1, 2, [lambda: scores(3, 1)])
    from_sibling(0, 0)
    from_sibling(0, 7)
    scores(0, 0)
    scores(0, 1)

    for e in range(NX):
        top = jnp.maximum(jnp.maximum(mq[0, e], mq[1, e]), jnp.maximum(mq[2, e], mq[3, e]))
        total = jnp.zeros((RESP, TOK), F32)
        for j in range(4):
            total = total + jnp.exp2((mq[j, e] - top) * SCALE) * lq[j, e]
        gstat[x, (x + e) % NX, 0] = top
        gstat[x, (x + e) % NX, 1] = total
    for d in range(1, NX):
        send(gstat.at[x], gstat.at[x], ssend.at[d], srecv.at[d], at_x(d))
    probe(0)
    ring_step(1, 3, [lambda: probe(1)])
    for d in range(1, NX):
        arrived(gstat.at[(x + NX - d) % NX], srecv.at[d])
    for e in range(NX):
        xx = (x + e) % NX
        tops = [gstat[i, xx, 0] for i in range(NX)]
        top = jnp.maximum(jnp.maximum(tops[0], tops[1]), jnp.maximum(tops[2], tops[3]))
        total = jnp.zeros((RESP, TOK), F32)
        for i in range(NX):
            total = total + jnp.exp2((tops[i] - top) * SCALE) * gstat[i, xx, 1]
        inverse = 1.0 / total
        for j in range(4):
            coef[e, j] = jnp.exp2((mq[j, e] - top) * SCALE) * inverse
    judged = jnp.zeros((RESP, 128), F32)
    for e in range(NX):
        dots = jnp.zeros((RESP, 128), F32)
        for j in range(4):
            dots = dots + coef[e, j] * sq[j, e]
        dots = jnp.sum(jnp.where(lane < lens[e], dots, 0.0), axis=1, keepdims=True)
        dots = jnp.broadcast_to(dots, (RESP, 128)) / lens[e].astype(F32)
        judged = judged + jnp.where(lane == (x + e) % NX, dots, 0.0)
    t1[z] = judged
    spread(0, t1, z, NZ, at_z)
    for number in range(8):
        from_sibling(1, number)

    def output(e, r):
        out = jnp.zeros((HEAD, TOK), F32)
        for j in range(4):
            vals = []
            for k in range(2):
                s = idsm[e, k, r]
                vals.append(vbuf[s // 2, s % 2, (quarter + j) % 4].reshape(HEAD, 128))
            part = jnp.dot(
                jnp.concatenate(vals, axis=1), pbuf[e, r, j], preferred_element_type=F32
            )
            out = out + part * coef[e, j, pl.ds(r, 1), :]
        return out

    def out_copy(e, r):
        if e == 2:
            return [
                remote(
                    obuf.at[2, rr], mbuf.at[rr], osend.at[2, rr], orecv.at[2, rr], at_x(d)
                )
                for rr, d in ((r, 1), (4 + r, 3))
            ]
        return remote(obuf.at[e, r], rbuf.at[4 - e, r], osend.at[e, r], orecv.at[4 - e, r], at_x(e))

    def opposite(r, carry):
        first, second = output(2, r), output(2, 4 + r)
        obuf[2, r] = first.astype(BF)
        obuf[2, 4 + r] = second.astype(BF)
        for copy in out_copy(2, r):
            copy.start()
        return carry

    def beside(r, carry):
        first, second = output(1, 4 + r), output(3, r)
        obuf[1, 4 + r] = first.astype(BF)
        obuf[3, r] = second.astype(BF)
        out_copy(1, 4 + r).start()
        out_copy(3, r).start()
        return carry

    def merged(r, carry):
        first, second = output(1, r), output(3, 4 + r)
        arrived(mbuf.at[r], orecv.at[2, r])
        arrived(mbuf.at[4 + r], orecv.at[2, 4 + r])
        first = first + mbuf[r].astype(F32)
        second = second + mbuf[4 + r].astype(F32)
        obuf[1, r] = first.astype(BF)
        obuf[3, 4 + r] = second.astype(BF)
        out_copy(1, r).start()
        out_copy(3, 4 + r).start()
        return carry

    def mine(r, carry):
        first, second = output(0, r), output(0, 4 + r)
        rbuf[0, r] = first.astype(BF)
        rbuf[0, 4 + r] = second.astype(BF)
        return carry

    lax.fori_loop(0, 4, opposite, 0, unroll=2)
    lax.fori_loop(0, 4, beside, 0, unroll=2)
    gather(0, t1, z, NZ)
    t2[y] = jnp.sum(t1[...], axis=0)
    spread(1, t2, y, NY, at_y)
    lax.fori_loop(0, 4, mine, 0, unroll=2)
    lax.fori_loop(0, 4, merged, 0, unroll=2)
    gather(1, t2, y, NY)
    t3[g] = jnp.sum(t2[...], axis=0)
    spread(2, t3, g, NG, at_g)

    token = lax.broadcasted_iota(jnp.int32, (HEAD, TOK), 1)

    def att_copy(r):
        return pltpu.make_async_copy(abuf.at[r], att_ref.at[r], asem.at[r])

    def combine(r):
        total = rbuf[0, r].astype(F32)
        for e in (1, 3):
            arrived(rbuf.at[e, r], orecv.at[e, r])
            total = total + rbuf[e, r].astype(F32)
        total = jnp.where(token < BLK * len_ref[r], total, 0.0).astype(BF)
        abuf[r] = jnp.transpose(total)
        att_copy(r).start()

    def combine_pair(r, carry):
        combine(r)
        combine(4 + r)
        return carry

    drain()
    lax.fori_loop(0, 4, combine_pair, 0)
    gather(2, t3, g, NG)
    flat = jnp.zeros((RESP, 128), F32)
    for i in range(NC):
        scored = t3[i] + t3[2 + i] + t3[4 + i] + t3[6 + i]
        for xx in range(NX):
            column = jnp.broadcast_to(scored[:, xx:xx + 1], (RESP, 128))
            flat = flat + jnp.where(lane == (xx * NC + i) * RESP + row, column, 0.0)
    flat = jnp.sum(flat, axis=0, keepdims=True)
    flat = flat - jnp.sum(flat, axis=1, keepdims=True) / (NG * RESP)
    rel_ref[...] = flat[:, :NG * RESP]

    def finish(r, carry):
        for copy in out_copy(2, r):
            copy.wait_send()
        for rr in (r, 4 + r):
            out_copy(1, rr).wait_send()
            out_copy(3, rr).wait_send()
            att_copy(rr).wait()
        return carry

    lax.fori_loop(0, 4, finish, 0)


def local(queries, keys, values, span_ids, lengths, judge):
    vmem = pl.BlockSpec(memory_space=pltpu.VMEM)
    smem = pl.BlockSpec(memory_space=pltpu.SMEM)
    hbm = pl.BlockSpec(memory_space=pl.ANY)
    dma = pltpu.SemaphoreType.DMA
    attended, relative = pl.pallas_call(
        kernel,
        out_shape=(
            jax.ShapeDtypeStruct((RESP, TOK, HEAD), BF),
            jax.ShapeDtypeStruct((1, NG * RESP), F32),
        ),
        in_specs=[hbm, hbm, hbm, hbm, smem, hbm],
        out_specs=(hbm, vmem),
        scratch_shapes=[
            pltpu.VMEM((NZ, 2, 2, POS, HEAD), BF),
            pltpu.VMEM((NZ, 2, 2, POS, HEAD), BF),
            pltpu.VMEM((NZ, 2, 2, POS, HEAD), BF),
            pltpu.VMEM((NZ, 2, 2, POS, HEAD), BF),
            pltpu.VMEM((NZ, 2, 4, 2, POS, 128), BF),
            pltpu.VMEM((128, NZ * HEAD), BF),
            pltpu.VMEM((NZ, 2, POS, 128), BF),
            pltpu.VMEM((NX, RESP, TOK, HEAD), BF),
            pltpu.VMEM((NX, 2, RESP), jnp.int32),
            pltpu.SMEM((NX, 2, RESP), jnp.int32),
            pltpu.VMEM((NX, RESP, 128), jnp.int32),
            pltpu.VMEM((NX, RESP, 4, 256, TOK), BF),
            pltpu.VMEM((4, NX, RESP, TOK), F32),
            pltpu.VMEM((4, NX, RESP, TOK), F32),
            pltpu.VMEM((NX, 4, RESP, TOK), F32),
            pltpu.VMEM((4, NX, RESP, TOK), F32),
            pltpu.VMEM((NX, NX, 2, RESP, TOK), F32),
            pltpu.VMEM((NX, RESP, HEAD, TOK), BF),
            pltpu.VMEM((RESP, HEAD, TOK), BF),
            pltpu.VMEM((NX, RESP, HEAD, TOK), BF),
            pltpu.VMEM((NZ * NY, HEAD), F32),
            pltpu.VMEM((NZ, NY, 128), F32),
            pltpu.VMEM((NZ, NY, 128), F32),
            pltpu.VMEM((NY, NZ, 128), F32),
            pltpu.VMEM((NY, NZ, 128), F32),
            pltpu.VMEM((NZ, 2, 4, 16, 128), BF),
            pltpu.VMEM((RESP, TOK, HEAD), BF),
            pltpu.VMEM((NZ, RESP, TOK), F32),
            pltpu.VMEM((NY, RESP, TOK), F32),
            pltpu.VMEM((NG, RESP, TOK), F32),
            dma((4,)),
            dma((2, NZ)),
            dma((2, NZ)),
            dma((2, 2, 4, 4)),
            dma((2, 2, 4, 4)),
            dma((2, 8, 4)),
            dma((2, 8, 4)),
            dma((NX, 2)),
            dma((NX, 2)),
            dma((NX,)),
            dma((NX,)),
            dma((NX,)),
            dma((NX,)),
            dma((2, 8)),
            dma((2, 8)),
            dma((NX,)),
            dma((NX,)),
            dma((NX, RESP)),
            dma((NX, RESP)),
            dma((RESP,)),
            dma((3, 8)),
            dma((3, 8)),
        ],
        compiler_params=pltpu.CompilerParams(
            collective_id=0, has_side_effects=True, vmem_limit_bytes=60 * 1024 * 1024
        ),
    )(queries, keys, values, span_ids.T, lengths, judge.reshape(NZ * NY, HEAD))
    return attended, relative.reshape(NG * RESP)


def solution(mesh):
    return jax.shard_map(
        local,
        mesh=mesh,
        in_specs=(
            P("resp", None, "ctx"),
            P("ctx", None),
            P("ctx", None),
            P("resp", None),
            P("resp"),
            P(),
        ),
        out_specs=(P("resp", None, "ctx"), P()),
        check_vma=False,
    )
```

```python
import math

import jax
import jax.numpy as jnp
from jax import lax
from jax.experimental import pallas as pl
from jax.experimental.pallas import tpu as pltpu
from jax.sharding import PartitionSpec as P

MESH = pl.DeviceIdType.MESH
NZ, NY, NX, NC = 8, 8, 4, 2
NG = NX * NC
HEAD = 128
TOK = 128
RESP = 8
BLK = 64
POS = 64
PIECES = (4, 2)
SCALE = math.log2(math.e) / math.sqrt(HEAD)
BF = jnp.bfloat16
F32 = jnp.float32


def kernel(
    q_ref, k_ref, v_ref, span_ref, len_ref, judge_ref,
    att_ref, rel_ref,
    kb0, kb1, kb2, kb3, vbuf, vstage, vtb, qbuf, idbuf, idsm, lens, pbuf, mq, lq, coef,
    sq, gstat, obuf, mbuf, rbuf, jbuf, vjs, vjr, vjt, vjf, vjb, abuf, t1, t2, t3,
    local_sem, sent_sem, zrecv, yrecv, crecv, qrecv, idrecv, jrecv, srecv, orecv, rrecv,
):
    n = lax.axis_index("ctx")
    g = lax.axis_index("resp")
    z, y = n // NY, n % NY
    x, c = g // NC, g % NC
    half, quarter = y // 4, y % 4
    kb = (kb0, kb1, kb2, kb3)

    def at_z(zz):
        return (zz * NY + y, g)

    def at_y(yy):
        return (z * NY + yy, g)

    def at_g(gg):
        return (n, gg)

    def at_x(d):
        return (n, ((x + d) % NX) * NC + c)

    sibling = at_g(x * NC + (1 - c))

    def remote(src, dst, ss, rs, dev):
        return pltpu.make_async_remote_copy(
            src_ref=src, dst_ref=dst, send_sem=ss, recv_sem=rs, device_id=dev, device_id_type=MESH
        )

    def send(src, dst, kind, rs, dev):
        remote(src, dst, sent_sem.at[kind], rs, dev).start()

    def arrived(dst, rs):
        remote(dst, dst, rs, rs, sibling).wait_recv()

    def all_sent(ref, kind):
        remote(ref, ref, sent_sem.at[kind], sent_sem.at[kind], sibling).wait_send()

    def block(w, zz):
        count = PIECES[w]
        width = NZ // count
        return (z // width + count - zz // width) % count

    rows = pl.ds(pl.multiple_of(x * 128, 128), 128)
    krows = pl.ds(pl.multiple_of(x * 128 + c * POS, POS), POS)

    def cols(zz):
        return pl.ds(pl.multiple_of(zz * HEAD, HEAD), HEAD)

    vload = pltpu.make_async_copy(v_ref.at[rows, :], vstage, local_sem.at[0])
    vload.start()
    pltpu.make_async_copy(k_ref.at[krows, cols(z)], kb0.at[z, half, c], zrecv.at[0, 0]).start()
    idload = pltpu.make_async_copy(span_ref, idbuf.at[0], local_sem.at[1])
    idload.start()
    qown = pltpu.make_async_copy(q_ref, qbuf.at[0], local_sem.at[2])
    qown.start()
    jload = pltpu.make_async_copy(judge_ref, jbuf, local_sem.at[3])
    jload.start()

    barrier = pltpu.get_barrier_semaphore()
    for d in range(1, NZ):
        pl.semaphore_signal(barrier, inc=1, device_id=at_z((z + d) % NZ), device_id_type=MESH)
    for d in range(1, NY):
        pl.semaphore_signal(barrier, inc=1, device_id=at_y((y + d) % NY), device_id_type=MESH)
    for d in range(1, NG):
        pl.semaphore_signal(barrier, inc=1, device_id=at_g((g + d) % NG), device_id_type=MESH)
    row = lax.broadcasted_iota(jnp.int32, (RESP, 128), 0)
    lane = lax.broadcasted_iota(jnp.int32, (RESP, 128), 1)
    own_lens = jnp.zeros((RESP, 128), jnp.int32)
    for r in range(RESP):
        own_lens = jnp.where(row == r, len_ref[r], own_lens)
    pl.semaphore_wait(barrier, NZ + NY + NG - 3)

    for d in (1, 7, 2, 6, 3, 5, 4):
        zz = (z + d) % NZ
        send(
            k_ref.at[krows, cols(zz)], kb0.at[z, half, c],
            0, zrecv.at[0, block(0, zz)], at_z(zz),
        )
    for i in range(2):
        for d in (1, 3):
            part = pl.ds(4 * i if d == 1 else 4 - 4 * i, 4)
            send(
                q_ref.at[part], qbuf.at[4 - d, part], 3, qrecv.at[4 - d, i], at_x(d)
            )
    vload.wait()
    for j in range(NZ):
        vtb[j] = jnp.transpose(vstage[:, j * HEAD:(j + 1) * HEAD]).reshape(2, POS, 128)
    pltpu.make_async_copy(vtb.at[z, c], vbuf.at[z, half, quarter, c], zrecv.at[1, 0]).start()
    for d in (1, 7, 2, 6, 3, 5, 4):
        zz = (z + d) % NZ
        send(
            vtb.at[zz, c], vbuf.at[z, half, quarter, c],
            0, zrecv.at[1, block(1, zz)], at_z(zz),
        )
    idload.wait()
    lens[0] = own_lens * BLK
    for d in (1, 3, 2):
        send(idbuf.at[0], idbuf.at[4 - d], 4, idrecv.at[0], at_x(d))
        send(lens.at[0], lens.at[4 - d], 5, idrecv.at[1], at_x(d))

    def chunk(w, j, zs, yy, cc):
        if w == 0:
            return kb[j % 4].at[zs, yy // 4, cc]
        return vbuf.at[zs, yy // 4, yy % 4, cc]

    def piece(w, j, i, cc):
        count = PIECES[w]
        width = NZ // count
        first = ((z // width + i) % count) * width
        return chunk(w, j, pl.ds(first, width), (y + j + NY) % NY, cc)

    def valid(w, way, t, i):
        return t < 3 or (i < PIECES[w] // 2) == (way == 0)

    def hop(w, way, t, i):
        count = PIECES[w]
        size = 3 * count + count // 2
        step = t * count + i if t < 3 else 3 * count + i % (count // 2)
        return (7 * PIECES[0] if w else 0) + way * size + step

    def to_next(w, way, t, i):
        j = -t if way == 0 else t
        count = PIECES[w]
        width = NZ // count
        first = ((z // width + i) % count) * width
        dst = chunk(w, j + (-1 if way == 0 else 1), pl.ds(first, width), (y + j + NY) % NY, c)
        dev = at_y((y + (1 if way == 0 else NY - 1)) % NY)
        send(piece(w, j, i, c), dst, 1, yrecv.at[hop(w, way, t, i)], dev)

    def to_sibling(w, j, i):
        ref = piece(w, j, i, c)
        send(ref, ref, 2, crecv.at[4 if w else j % 4], sibling)

    def own_chunk(w):
        for i in range(PIECES[w]):
            arrived(piece(w, 0, i, c), zrecv.at[w, i])
            for way in range(2):
                to_next(w, way, 0, i)
            to_sibling(w, 0, i)

    def ring_step(w, t, work=()):
        work = list(work)
        for i in range(PIECES[w]):
            if i % 2 == 0 and work:
                work.pop(0)()
            for way in range(2):
                if not valid(w, way, t, i):
                    continue
                j = -1 - t if way == 0 else 1 + t
                arrived(piece(w, j, i, c), yrecv.at[hop(w, way, t, i)])
                if t < 3 and valid(w, way, t + 1, i):
                    to_next(w, way, t + 1, i)
                to_sibling(w, j, i)

    def from_sibling(j):
        arrived(kb[j].at[:, :, 1 - c], crecv.at[j])

    def forward_queries():
        for d in (1, 3):
            part = pl.ds(4 if d == 1 else 0, 4)
            arrived(qbuf.at[d, part], qrecv.at[d, 0])
            send(
                qbuf.at[d, part], qbuf.at[2, part], 3, qrecv.at[2, d // 2],
                at_x(4 - d),
            )

    def wait_queries():
        qown.wait()
        for d in (1, 3):
            arrived(qbuf.at[d, pl.ds(0 if d == 1 else 4, 4)], qrecv.at[d, 1])
            arrived(qbuf.at[2, pl.ds(4 if d == 1 else 0, 4)], qrecv.at[2, d // 2])
        arrived(idbuf.at[pl.ds(0, 3)], idrecv.at[0])
        arrived(lens.at[pl.ds(0, 3)], idrecv.at[1])
        ids = pltpu.make_async_copy(idbuf, idsm, local_sem.at[1])
        ids.start()
        ids.wait()

    def judge_values():
        jload.wait()
        for j in range(NZ):
            rest = jbuf[j * NY:(j + 1) * NY, :]
            terms = []
            for _ in range(3):
                terms.append(rest.astype(BF).astype(F32))
                rest = rest - terms[-1]
            terms.append(jnp.zeros((NY, HEAD), F32))
            dots = jnp.dot(
                jnp.concatenate(terms, axis=0).astype(BF), vtb[j].reshape(HEAD, 128),
                preferred_element_type=F32,
            )
            vjs[j] = dots[:NY] + dots[NY:2 * NY] + dots[2 * NY:3 * NY]
        vjr[z] = vjs[z]
        for d in range(1, NZ):
            zz = (z + d) % NZ
            send(vjs.at[zz], vjr.at[z], 6, jrecv.at[0], at_z(zz))

    def judged_to_heads():
        arrived(vjr.at[pl.ds(0, NZ - 1)], jrecv.at[0])
        for yy in range(NY):
            vjt[yy] = vjr[:, yy, :]
        vjf[y] = vjt[y]
        for d in range(1, NY):
            yy = (y + d) % NY
            send(vjt.at[yy], vjf.at[y], 7, jrecv.at[1], at_y(yy))

    def judged_values():
        arrived(vjf.at[pl.ds(0, NY - 1)], jrecv.at[1])
        line = lax.broadcasted_iota(jnp.int32, (16, 128), 0)

        def one(zz, carry):
            for yy in range(NY):
                exact = jnp.broadcast_to(vjf[yy, pl.ds(zz, 1), :], (16, 128))
                high = exact.astype(BF).astype(F32)
                j = 2 * ((yy % 4 - quarter + 4) % 4)
                tile = jnp.where(line == j, high, jnp.where(line == j + 1, exact - high, 0.0))
                vjb[zz, yy // 4, yy % 4] = tile.astype(BF)
            return carry

        lax.fori_loop(0, NZ, one, 0)

    def scores(j, part):
        def one(item, carry):
            e, r = item // RESP, item % RESP
            keys = []
            for k in range(2):
                s = idsm[e, k, r]
                keys.append(kb[j][s // 2, s % 2].reshape(128, HEAD))
            raw = lax.dot_general(
                jnp.concatenate(keys, axis=0), qbuf[e, r], (((1,), (1,)), ((), ())),
                preferred_element_type=F32,
            )
            top = jnp.max(raw, axis=0, keepdims=True)
            expo = jnp.exp2((raw - top) * SCALE)
            pbuf[e, r, j] = expo.astype(BF)
            mq[j, e, pl.ds(r, 1), :] = top
            lq[j, e, pl.ds(r, 1), :] = jnp.sum(expo, axis=0, keepdims=True)
            return carry

        lax.fori_loop(16 * part, 16 * part + 16, one, 0, unroll=8)

    def both(j):
        return [lambda: scores(j, 0), lambda: scores(j, 1)]

    def spread(number, buf, own, size, where):
        for d in range(1, size):
            send(
                buf.at[own], buf.at[own], 9 + number, rrecv.at[number], where((own + d) % size)
            )

    def gather(number, buf):
        arrived(buf.at[pl.ds(0, 7)], rrecv.at[number])

    def probe(part):
        def one(item, carry):
            e, r = item // RESP, item % RESP
            probes = []
            for j in range(4):
                for k in range(2):
                    s = idsm[e, k, r]
                    probes.append(vjb[s // 2, s % 2, (quarter + j) % 4])
            dots = jnp.dot(
                jnp.concatenate(probes, axis=1), pbuf[e, r].reshape(1024, TOK),
                preferred_element_type=F32,
            )
            for j in range(4):
                sq[j, e, pl.ds(r, 1), :] = dots[2 * j:2 * j + 1] + dots[2 * j + 1:2 * j + 2]
            return carry

        lax.fori_loop(16 * part, 16 * part + 16, one, 0, unroll=4)

    own_chunk(0)
    forward_queries()
    ring_step(0, 0)
    judge_values()
    own_chunk(1)
    ring_step(0, 1)
    wait_queries()
    ring_step(1, 0)
    from_sibling(2)
    ring_step(0, 2, both(2))
    judged_to_heads()
    ring_step(1, 1)
    from_sibling(1)
    from_sibling(3)
    ring_step(0, 3, both(1))
    scores(3, 0)
    ring_step(1, 2, [lambda: scores(3, 1)])
    from_sibling(0)
    scores(0, 0)
    scores(0, 1)

    for e in range(NX):
        top = jnp.maximum(jnp.maximum(mq[0, e], mq[1, e]), jnp.maximum(mq[2, e], mq[3, e]))
        total = jnp.zeros((RESP, TOK), F32)
        for j in range(4):
            total = total + jnp.exp2((mq[j, e] - top) * SCALE) * lq[j, e]
        gstat[x, (x + e) % NX, 0] = top
        gstat[x, (x + e) % NX, 1] = total
    for d in range(1, NX):
        send(gstat.at[x], gstat.at[x], 8, srecv.at[0], at_x(d))
    judged_values()
    probe(0)
    ring_step(1, 3, [lambda: probe(1)])
    arrived(gstat.at[pl.ds(0, 3)], srecv.at[0])
    for e in range(NX):
        xx = (x + e) % NX
        tops = [gstat[i, xx, 0] for i in range(NX)]
        top = jnp.maximum(jnp.maximum(tops[0], tops[1]), jnp.maximum(tops[2], tops[3]))
        total = jnp.zeros((RESP, TOK), F32)
        for i in range(NX):
            total = total + jnp.exp2((tops[i] - top) * SCALE) * gstat[i, xx, 1]
        inverse = 1.0 / total
        for j in range(4):
            coef[e, j] = jnp.exp2((mq[j, e] - top) * SCALE) * inverse
    judged = jnp.zeros((RESP, 128), F32)
    for e in range(NX):
        dots = jnp.zeros((RESP, 128), F32)
        for j in range(4):
            dots = dots + coef[e, j] * sq[j, e]
        dots = jnp.sum(jnp.where(lane < lens[e], dots, 0.0), axis=1, keepdims=True)
        dots = jnp.broadcast_to(dots, (RESP, 128)) / lens[e].astype(F32)
        judged = judged + jnp.where(lane == (x + e) % NX, dots, 0.0)
    t1[z] = judged
    spread(0, t1, z, NZ, at_z)
    arrived(vbuf.at[:, :, :, 1 - c], crecv.at[4])

    def output(e, r):
        out = jnp.zeros((HEAD, TOK), F32)
        for j in range(4):
            vals = []
            for k in range(2):
                s = idsm[e, k, r]
                vals.append(vbuf[s // 2, s % 2, (quarter + j) % 4].reshape(HEAD, 128))
            part = jnp.dot(
                jnp.concatenate(vals, axis=1), pbuf[e, r, j], preferred_element_type=F32
            )
            out = out + part * coef[e, j, pl.ds(r, 1), :]
        return out

    def out_send(e, r):
        if e == 2:
            send(obuf.at[2, r], mbuf.at[r], 12, orecv.at[r], at_x(1))
            send(obuf.at[2, 4 + r], mbuf.at[4 + r], 12, orecv.at[r], at_x(3))
        else:
            send(obuf.at[e, r], rbuf.at[4 - e, r], 12, orecv.at[4 + r % 4], at_x(e))

    def opposite(r, carry):
        first, second = output(2, r), output(2, 4 + r)
        obuf[2, r] = first.astype(BF)
        obuf[2, 4 + r] = second.astype(BF)
        out_send(2, r)
        return carry

    def beside(r, carry):
        first, second = output(1, 4 + r), output(3, r)
        obuf[1, 4 + r] = first.astype(BF)
        obuf[3, r] = second.astype(BF)
        out_send(1, 4 + r)
        out_send(3, r)
        return carry

    def merged(r, carry):
        first, second = output(1, r), output(3, 4 + r)
        arrived(mbuf.at[pl.ds(0, 2)], orecv.at[r])
        first = first + mbuf[r].astype(F32)
        second = second + mbuf[4 + r].astype(F32)
        obuf[1, r] = first.astype(BF)
        obuf[3, 4 + r] = second.astype(BF)
        out_send(1, r)
        out_send(3, 4 + r)
        return carry

    def mine(r, carry):
        first, second = output(0, r), output(0, 4 + r)
        rbuf[0, r] = first.astype(BF)
        rbuf[0, 4 + r] = second.astype(BF)
        return carry

    lax.fori_loop(0, 4, opposite, 0, unroll=2)
    lax.fori_loop(0, 4, beside, 0, unroll=2)
    gather(0, t1)
    t2[y] = jnp.sum(t1[...], axis=0)
    spread(1, t2, y, NY, at_y)
    lax.fori_loop(0, 4, mine, 0, unroll=2)
    lax.fori_loop(0, 4, merged, 0, unroll=2)
    gather(1, t2)
    t3[g] = jnp.sum(t2[...], axis=0)
    spread(2, t3, g, NG, at_g)

    token = lax.broadcasted_iota(jnp.int32, (HEAD, TOK), 1)

    def combine(r):
        total = rbuf[0, r].astype(F32)
        for e in (1, 3):
            total = total + rbuf[e, r].astype(F32)
        total = jnp.where(token < BLK * len_ref[r], total, 0.0).astype(BF)
        abuf[r] = jnp.transpose(total)
        pltpu.make_async_copy(abuf.at[r], att_ref.at[r], local_sem.at[4]).start()

    def combine_pair(r, carry):
        arrived(rbuf.at[pl.ds(0, 2), pl.ds(0, 2)], orecv.at[4 + r])
        combine(r)
        combine(4 + r)
        return carry

    for ref, kind in (
        (vtb.at[pl.ds(0, 7)], 0), (vbuf.at[pl.ds(0, 7)], 1), (vbuf, 2), (qbuf.at[pl.ds(0, 3)], 3),
        (idbuf.at[pl.ds(0, 3)], 4), (lens.at[pl.ds(0, 3)], 5), (vjs.at[pl.ds(0, 7)], 6),
        (vjt.at[pl.ds(0, 7)], 7), (gstat.at[pl.ds(0, 3)], 8), (t1.at[pl.ds(0, 7)], 9),
        (t2.at[pl.ds(0, 7)], 10),
    ):
        all_sent(ref, kind)
    lax.fori_loop(0, 4, combine_pair, 0)
    gather(2, t3)
    flat = jnp.zeros((RESP, 128), F32)
    for i in range(NC):
        scored = t3[i] + t3[2 + i] + t3[4 + i] + t3[6 + i]
        for xx in range(NX):
            column = jnp.broadcast_to(scored[:, xx:xx + 1], (RESP, 128))
            flat = flat + jnp.where(lane == (xx * NC + i) * RESP + row, column, 0.0)
    flat = jnp.sum(flat, axis=0, keepdims=True)
    flat = flat - jnp.sum(flat, axis=1, keepdims=True) / (NG * RESP)
    rel_ref[...] = flat[:, :NG * RESP]
    all_sent(t3.at[pl.ds(0, 7)], 11)
    all_sent(obuf.at[pl.ds(1, 3)], 12)
    pltpu.make_async_copy(abuf, att_ref, local_sem.at[4]).wait()


def local(queries, keys, values, span_ids, lengths, judge):
    vmem = pl.BlockSpec(memory_space=pltpu.VMEM)
    smem = pl.BlockSpec(memory_space=pltpu.SMEM)
    hbm = pl.BlockSpec(memory_space=pl.ANY)
    dma = pltpu.SemaphoreType.DMA
    attended, relative = pl.pallas_call(
        kernel,
        out_shape=(
            jax.ShapeDtypeStruct((RESP, TOK, HEAD), BF),
            jax.ShapeDtypeStruct((1, NG * RESP), F32),
        ),
        in_specs=[hbm, hbm, hbm, hbm, smem, hbm],
        out_specs=(hbm, vmem),
        scratch_shapes=[
            pltpu.VMEM((NZ, 2, 2, POS, HEAD), BF),
            pltpu.VMEM((NZ, 2, 2, POS, HEAD), BF),
            pltpu.VMEM((NZ, 2, 2, POS, HEAD), BF),
            pltpu.VMEM((NZ, 2, 2, POS, HEAD), BF),
            pltpu.VMEM((NZ, 2, 4, 2, POS, 128), BF),
            pltpu.VMEM((128, NZ * HEAD), BF),
            pltpu.VMEM((NZ, 2, POS, 128), BF),
            pltpu.VMEM((NX, RESP, TOK, HEAD), BF),
            pltpu.VMEM((NX, 2, RESP), jnp.int32),
            pltpu.SMEM((NX, 2, RESP), jnp.int32),
            pltpu.VMEM((NX, RESP, 128), jnp.int32),
            pltpu.VMEM((NX, RESP, 4, 256, TOK), BF),
            pltpu.VMEM((4, NX, RESP, TOK), F32),
            pltpu.VMEM((4, NX, RESP, TOK), F32),
            pltpu.VMEM((NX, 4, RESP, TOK), F32),
            pltpu.VMEM((4, NX, RESP, TOK), F32),
            pltpu.VMEM((NX, NX, 2, RESP, TOK), F32),
            pltpu.VMEM((NX, RESP, HEAD, TOK), BF),
            pltpu.VMEM((RESP, HEAD, TOK), BF),
            pltpu.VMEM((NX, RESP, HEAD, TOK), BF),
            pltpu.VMEM((NZ * NY, HEAD), F32),
            pltpu.VMEM((NZ, NY, 128), F32),
            pltpu.VMEM((NZ, NY, 128), F32),
            pltpu.VMEM((NY, NZ, 128), F32),
            pltpu.VMEM((NY, NZ, 128), F32),
            pltpu.VMEM((NZ, 2, 4, 16, 128), BF),
            pltpu.VMEM((RESP, TOK, HEAD), BF),
            pltpu.VMEM((NZ, RESP, TOK), F32),
            pltpu.VMEM((NY, RESP, TOK), F32),
            pltpu.VMEM((NG, RESP, TOK), F32),
            dma((5,)),
            dma((13,)),
            dma((2, 4)),
            dma((7 * (PIECES[0] + PIECES[1]),)),
            dma((5,)),
            dma((NX, 2)),
            dma((2,)),
            dma((2,)),
            dma((1,)),
            dma((8,)),
            dma((3,)),
        ],
        compiler_params=pltpu.CompilerParams(
            collective_id=0, has_side_effects=True, vmem_limit_bytes=60 * 1024 * 1024
        ),
    )(queries, keys, values, span_ids.T, lengths, judge.reshape(NZ * NY, HEAD))
    return attended, relative.reshape(NG * RESP)


def solution(mesh):
    return jax.shard_map(
        local,
        mesh=mesh,
        in_specs=(
            P("resp", None, "ctx"),
            P("ctx", None),
            P("ctx", None),
            P("resp", None),
            P("resp"),
            P(),
        ),
        out_specs=(P("resp", None, "ctx"), P()),
        check_vma=False,
    )
```
